32 devices in a mesh: chan: 8 (over z, y), ctx: 4 (over x, core).
Axes of the slice: x: 2, y: 2, z: 4, core: 2. Of those that a mesh axis runs over, the one named last changes fastest.
Arguments:
- query_in: bfloat16 [6144, 8192], P('ctx', 'chan'), may hold values from -6 to 6
- key_in: bfloat16 [6144, 8192], P('ctx', 'chan'), may hold values from -6 to 6
- value_in: bfloat16 [6144, 8192], P('ctx', 'chan'), may hold values from -6 to 6
- short_filter: float32 [3, 3, 8192], P(None, None, 'chan'), may hold values from -3.5 to 3.5
- residue: float32 [8192, 16], P('chan'), may hold values from -1.5 to 1.5
- decay_rate: float32 [8192, 16], P('chan'), may hold values from 3.25520833e-05 to 0.0333333333, as said below
- skip_gain: float32 [8192], P('chan'), may hold values from -4 to 4
- out_weight: bfloat16 [8192, 8192], P('ctx', 'chan'), may hold values from -0.0625 to 0.0625
Outputs:
- mixed_out: bfloat16 [6144, 8192], P('ctx', 'chan')
The draws below stay inside these ranges and needn't reach their ends.
Inputs may be any that keep to these rules, and one draw needn't show every extreme that they name: `decay_rate`: rates of the filter's modes.
All inputs are finite; a program needn't handle non-finite values.
Results may differ from the reference program's by a relative error of at most 0.0051.
Values may be sent and summed in bfloat16 or wider, within the bound.
A program may use at most 256 MiB of HBM per device.

```python
import math
import jax
import jax.numpy as jnp
from jax import lax

D = 8192
STATE = 16
SHORT = 3
LENGTH = 6144


def draw_decay_rate(key, part):
    key_mask = jax.random.fold_in(key, 11)
    key_slow = jax.random.fold_in(key, 12)
    key_fast = jax.random.fold_in(key, 13)
    slow_share = 0.5
    slow_mask = jax.random.bernoulli(key_mask, slow_share, (D, STATE))
    draw_slow = jax.random.uniform(key_slow, (D, STATE), jnp.float32)
    draw_fast = jax.random.uniform(key_fast, (D, STATE), jnp.float32)
    slow_low = math.log(0.2 / LENGTH)
    slow_high = math.log(2.0 / LENGTH)
    fast_high = math.log(1.0 / 30.0)
    slow_rate = jnp.exp(slow_low + draw_slow * (slow_high - slow_low))
    fast_rate = jnp.exp(slow_high + draw_fast * (fast_high - slow_high))
    return jnp.where(slow_mask, slow_rate, fast_rate).astype(jnp.float32)


def block_levels(key, dims, pieces, least, high):
    factor_of, own = 1.0, jax.random.fold_in(key, 6)
    for position, shards_of in pieces:
        heights = jnp.exp(jax.random.uniform(jax.random.fold_in(own, position), (shards_of,), jnp.float32, least / len(pieces), high / len(pieces)))
        factor_of = factor_of * jnp.repeat(heights, dims[position] // shards_of).reshape([-1 if axis == position else 1 for axis in range(len(dims))])
    return factor_of


def noise(own_key, extent, spread, reach, pieces=(), dtype=jnp.bfloat16):
    drawn = spread * jax.random.normal(own_key, extent, jnp.float32)
    if pieces:
        drawn = drawn * block_levels(own_key, extent, pieces, -0.22, 0.18)
    return jnp.clip(drawn, -reach, reach).astype(dtype)


def setup_inputs(seed: int = 0) -> dict:
    seeds = jax.random.split(jax.random.key(seed), 9)
    query_in = noise(seeds[0], (LENGTH, D), 1.0, 6.0, ((0, 4), (1, 8)))
    key_in = noise(seeds[1], (LENGTH, D), 1.0, 6.0, ((0, 4), (1, 8)))
    value_in = noise(seeds[2], (LENGTH, D), 1.0, 6.0, ((0, 4), (1, 8)))
    short_filter = noise(seeds[3], (3, SHORT, D), SHORT ** -0.5, 3.5, ((2, 8),), jnp.float32)
    residue = noise(seeds[4], (D, STATE), 0.25, 1.5, ((0, 8),), jnp.float32)
    decay_rate = draw_decay_rate(jax.random.fold_in(seeds[8], 71), 0)
    skip_gain = noise(seeds[6], (D,), 1.0, 4.0, ((0, 8),), jnp.float32)
    out_weight = noise(seeds[7], (D, D), D ** -0.5, 0.0625, ((0, 4), (1, 8)))
    return {"query_in": query_in, "key_in": key_in, "value_in": value_in, "short_filter": short_filter, "residue": residue, "decay_rate": decay_rate, "skip_gain": skip_gain, "out_weight": out_weight}


def short_pass(padded, short_filter, length_all):
    tap_count = short_filter.shape[1]
    result = jnp.zeros((padded.shape[0], length_all, padded.shape[2]), jnp.float32)
    for tap_index in range(tap_count):
        begin = tap_count - 1 - tap_index
        result = result + short_filter[:, tap_index, None, :] * padded[:, begin:begin + length_all, :]
    return result

def reference(query_in, key_in, value_in, short_filter, residue, decay_rate, skip_gain, out_weight):
    stacked = jnp.stack([query_in, key_in, value_in]).astype(jnp.float32)
    padded = jnp.pad(stacked, ((0, 0), (SHORT - 1, 0), (0, 0)))
    shorted = short_pass(padded, short_filter, LENGTH)
    drive_in = shorted[1] * shorted[2]
    decay = jnp.exp(-decay_rate)
    mode_gain = residue * jnp.sqrt(decay_rate)

    def advance(state, column):
        state = decay * state + column[:, None]
        return (state, lax.optimization_barrier(jnp.sum(mode_gain * state, axis=1)))
    initial = jnp.zeros(decay_rate.shape, jnp.float32)
    final_state, mode_conv = lax.scan(advance, initial, drive_in)
    gated_out = (shorted[0] * (mode_conv + skip_gain[None, :] * drive_in)).astype(jnp.bfloat16)
    return jnp.dot(gated_out, out_weight, preferred_element_type=jnp.float32).astype(jnp.bfloat16)
```

```python
import functools

import jax
import jax.numpy as jnp
from jax import lax
from jax.experimental import pallas as pl
from jax.experimental.pallas import tpu as pltpu
from jax.sharding import PartitionSpec as P

MESH = pl.DeviceIdType.MESH
SEGMENTS = 8
LANES = 128
HALO = 8
PIECES = 4
MIB = 1024 * 1024


def short_stream(x_ref, edge_ref, taps, padded, result_of, length):
    padded[HALO - edge_ref.shape[0] : HALO, :] = edge_ref[...].astype(jnp.float32)
    for seg in range(SEGMENTS):
        at = seg * length
        padded[HALO + at : HALO + at + length, :] = x_ref[at : at + length, :].astype(jnp.float32)
    for seg in range(SEGMENTS):
        at = seg * length
        total = None
        for tap in range(taps.shape[0]):
            begin = HALO + at - tap
            term = taps[tap : tap + 1, :] * padded[begin : begin + length, :]
            total = term if total is None else total + term
        result_of(at, total)


def write_to(ref, length):
    def put(at, value):
        ref[at : at + length, :] = value

    return put


def multiply_into(ref, length):
    def put(at, value):
        ref[at : at + length, :] = ref[at : at + length, :] * value

    return put


def ends_kernel(k_ref, v_ref, edge_ref, taps_ref, rate_ref, seg_ref, end_ref, padded, drive):
    tokens = k_ref.shape[0]
    modes = rate_ref.shape[0]
    length = tokens // SEGMENTS
    short_stream(k_ref, edge_ref.at[1], taps_ref.at[1], padded, write_to(drive, length), length)
    short_stream(v_ref, edge_ref.at[2], taps_ref.at[2], padded, multiply_into(drive, length), length)
    decay = jnp.exp(-rate_ref[...])
    decays = [jnp.broadcast_to(decay[n : n + 1, :], (SEGMENTS, LANES)) for n in range(modes)]
    unroll = 4

    def steps(block, states):
        for inner in range(unroll):
            u = drive[pl.ds(block * unroll + inner, SEGMENTS, stride=length), :]
            states = tuple(decays[n] * states[n] + u for n in range(modes))
        return states

    zero = jnp.zeros((SEGMENTS, LANES), jnp.float32)
    states = lax.fori_loop(0, length // unroll, steps, (zero,) * modes)
    for n in range(modes):
        seg_ref[n] = states[n]
    span = jnp.exp(-rate_ref[...] * float(length))
    total = jnp.zeros((modes, LANES), jnp.float32)
    for seg in range(SEGMENTS):
        total = span * total + seg_ref[:, seg, :]
    end_ref[...] = total


def gated_kernel(
    q_ref, k_ref, v_ref, edge_ref, taps_ref, rate_ref, gain_ref, skip_ref, seg_ref, carry_ref,
    out_ref, padded, drive, query, conv, starts,
):
    tokens = k_ref.shape[0]
    modes = rate_ref.shape[0]
    length = tokens // SEGMENTS
    short_stream(q_ref, edge_ref.at[0], taps_ref.at[0], padded, write_to(query, length), length)
    short_stream(k_ref, edge_ref.at[1], taps_ref.at[1], padded, write_to(drive, length), length)
    short_stream(v_ref, edge_ref.at[2], taps_ref.at[2], padded, multiply_into(drive, length), length)
    span = jnp.exp(-rate_ref[...] * float(length))
    state = carry_ref[...]
    for seg in range(SEGMENTS):
        starts[:, seg, :] = state
        state = span * state + seg_ref[:, seg, :]
    decay = jnp.exp(-rate_ref[...])
    gain = gain_ref[...]
    decays = [jnp.broadcast_to(decay[n : n + 1, :], (SEGMENTS, LANES)) for n in range(modes)]
    gains = [jnp.broadcast_to(gain[n : n + 1, :], (SEGMENTS, LANES)) for n in range(modes)]
    unroll = 4

    def steps(block, states):
        for inner in range(unroll):
            at = block * unroll + inner
            u = drive[pl.ds(at, SEGMENTS, stride=length), :]
            states = tuple(decays[n] * states[n] + u for n in range(modes))
            even, odd = gains[0] * states[0], gains[1] * states[1]
            for n in range(2, modes, 2):
                even = even + gains[n] * states[n]
                odd = odd + gains[n + 1] * states[n + 1]
            conv[pl.ds(at, SEGMENTS, stride=length), :] = even + odd
        return states

    lax.fori_loop(0, length // unroll, steps, tuple(starts[n] for n in range(modes)))
    for seg in range(SEGMENTS):
        at = seg * length
        rows = slice(at, at + length)
        out_ref[rows, :] = (
            query[rows, :] * (conv[rows, :] + skip_ref[...] * drive[rows, :])
        ).astype(out_ref.dtype)


def route(shards):
    line = shards // 2
    plans = []
    for me in range(shards):
        z, y = me // 2, me % 2
        events = []
        for shard in range(shards):
            from_z, from_y = shard // 2, shard % 2
            apart = abs(from_z - z)
            halves = []
            for half in range(2):
                if from_y == y:
                    low = z > 0 and from_z >= z
                    high = z < line - 1 and from_z <= z
                    pair = not (half == 1 and apart == 1)
                    key = float(apart)
                else:
                    low = z > 0 and apart == 0 and half == 1
                    high = z < line - 1 and apart == 0 and half == 1
                    pair = False
                    key = apart + 0.5
                halves.append((low, high, pair))
            events.append((key, shard, halves))
        events.sort(key=lambda e: (e[0], e[1]))
        plans.append([
            (shard, [int(a) + 2 * int(b) + 4 * int(c) for a, b, c in halves])
            for _, shard, halves in events
        ])
    return plans


def pick(values, index):
    result = jnp.int32(values[0])
    for position in range(1, len(values)):
        result = jnp.where(index == position, values[position], result)
    return result


def mix_kernel(shards, blocks, g_ref, w_ref, out_ref, held, weight, total, own_sem, wown_sem, send_sem, recv_sem, wsend_sem, wrecv_sem):
    tokens, width = g_ref.shape
    depth, columns = w_ref.shape
    rows = tokens // PIECES
    me = lax.axis_index("chan")
    ctx = lax.axis_index("ctx")
    line = shards // 2
    z, y = me // 2, me % 2
    plans = route(shards)
    codes = [
        pick([plan[k][0] + shards * (plan[k][1][0] + 8 * plan[k][1][1]) for plan in plans], me)
        for k in range(shards)
    ]
    targets = (me - 2, me + 2, me + 1 - 2 * y)

    def flip(by):
        result, bit = ctx, 1
        while bit <= by:
            if by & bit:
                result = result + bit * (1 - 2 * ((ctx // bit) % 2))
            bit *= 2
        return result

    def block_of(index):
        return weight.at[pl.ds(pl.multiple_of(index * depth, depth), depth), :]

    own_copy = pltpu.make_async_copy(g_ref, held.at[me], own_sem)
    own_copy.start()
    weight_copy = pltpu.make_async_copy(w_ref, block_of(ctx), wown_sem)
    weight_copy.start()

    barrier = pltpu.get_barrier_semaphore()

    @pl.when(z > 0)
    def _():
        pl.semaphore_signal(barrier, inc=1, device_id={"chan": targets[0]}, device_id_type=MESH)

    @pl.when(z < line - 1)
    def _():
        pl.semaphore_signal(barrier, inc=1, device_id={"chan": targets[1]}, device_id_type=MESH)

    pl.semaphore_signal(barrier, inc=1, device_id={"chan": targets[2]}, device_id_type=MESH)
    partners = [1] + list(range(2, blocks, 2))
    for by in partners:
        pl.semaphore_signal(barrier, inc=1, device_id={"ctx": flip(by)}, device_id_type=MESH)
    lines = jnp.where(z > 0, 1, 0) + jnp.where(z < line - 1, 1, 0)
    pl.semaphore_wait(barrier, lines + 1 + len(partners))

    def piece_copy(shard, piece, way):
        part = held.at[shard, pl.ds(pl.multiple_of(piece * rows, rows), rows), :]
        return pltpu.make_async_remote_copy(
            src_ref=part,
            dst_ref=part,
            send_sem=send_sem.at[shard, piece, way],
            recv_sem=recv_sem.at[shard, piece],
            device_id={"chan": targets[way]},
            device_id_type=MESH,
        )

    def weight_send(block, by, slot):
        return pltpu.make_async_remote_copy(
            src_ref=block_of(block),
            dst_ref=block_of(block),
            send_sem=wsend_sem.at[slot],
            recv_sem=wrecv_sem.at[block],
            device_id={"ctx": flip(by)},
            device_id_type=MESH,
        )

    def onward(code, piece, act):
        shard = code % shards
        flags = code // shards
        flags = jnp.where(piece < PIECES // 2, flags % 8, flags // 8)
        for way, bit in ((0, flags % 2), (1, (flags // 2) % 2), (2, flags // 4)):

            @pl.when(bit == 1)
            def _(way=way):
                act(piece_copy(shard, piece, way))

    own_copy.wait()

    @pl.loop(0, PIECES)
    def _(piece):
        onward(codes[0], piece, lambda copy: copy.start())

    weight_copy.wait()
    first_sends = [weight_send(ctx, by, slot) for slot, by in enumerate(partners)]
    for copy in first_sends:
        copy.start()

    def zero_rows(at):
        total[pl.ds(pl.multiple_of(at * 64, 64), 64), :] = jnp.zeros((64, columns), jnp.float32)

    pl.loop(0, tokens // 64)(zero_rows)

    def arrive(code, piece):
        piece_copy(code % shards, piece, 2).wait_recv()
        onward(code, piece, lambda copy: copy.start())

    half = shards // 2
    later_sends = []
    for k in range(1, half):
        code = codes[k]
        if k < half - 1:

            @pl.loop(0, PIECES)
            def _(piece, code=code):
                arrive(code, piece)
        else:

            @pl.loop(0, PIECES // 2)
            def _(piece, code=code):
                arrive(code, piece)

            for by in partners[1:]:
                block = flip(by)
                weight_send(block, 1, 0).wait_recv()
                copy = weight_send(block, 1, len(partners) + len(later_sends))
                copy.start()
                later_sends.append(copy)

            @pl.loop(PIECES // 2, PIECES)
            def _(piece, code=code):
                arrive(code, piece)

    weight_send(flip(1), 1, 0).wait_recv()
    for by in partners[1:]:
        weight_send(flip(by + 1), 1, 0).wait_recv()

    tile = 256

    def multiply(shard, piece):
        here = pl.ds(pl.multiple_of(piece * rows, rows), rows)
        deep = pl.ds(pl.multiple_of(shard * width, width), width)

        @pl.loop(0, columns // tile)
        def _(part):
            cols = pl.ds(pl.multiple_of(part * tile, tile), tile)
            total[here, cols] += jnp.dot(
                held[shard, here, :], weight[deep, cols], preferred_element_type=jnp.float32
            )

    @pl.loop(half, shards)
    def _(k):
        code = pick(codes, k)
        earlier = pick(codes, 2 * (k - half)) % shards
        later = pick(codes, 2 * (k - half) + 1) % shards

        @pl.loop(0, PIECES)
        def _(piece):
            arrive(code, piece)
            multiply(earlier, piece)
            multiply(later, piece)

    def round_rows(at):
        here = pl.ds(pl.multiple_of(at * 64, 64), 64)
        out_ref[here, :] = total[here, :].astype(out_ref.dtype)

    pl.loop(0, tokens // 64)(round_rows)

    @pl.loop(0, shards)
    def _(k):
        code = pick(codes, k)

        @pl.loop(0, PIECES)
        def _(piece):
            onward(code, piece, lambda copy: copy.wait_send())

    for copy in first_sends + later_sends:
        copy.wait_send()


def on_device(query_in, key_in, value_in, short_filter, residue, decay_rate, skip_gain, out_weight):
    tokens, channels = query_in.shape
    tap_count = short_filter.shape[1]
    modes = decay_rate.shape[1]
    shards = lax.axis_size("chan")
    blocks = lax.axis_size("ctx")
    position = lax.axis_index("ctx")
    edge = jnp.stack([x[tokens - (tap_count - 1) :, :] for x in (query_in, key_in, value_in)])
    edge = lax.ppermute(edge, "ctx", [(i, i + 1) for i in range(blocks - 1)])
    rate = decay_rate.T
    gain = (residue * jnp.sqrt(decay_rate)).T
    skip = skip_gain[None, :]

    stream = pl.BlockSpec((tokens, LANES), lambda i: (0, i))
    edges = pl.BlockSpec((3, tap_count - 1, LANES), lambda i: (0, 0, i))
    taps = pl.BlockSpec((3, tap_count, LANES), lambda i: (0, 0, i))
    mode = pl.BlockSpec((modes, LANES), lambda i: (0, i))
    segs = pl.BlockSpec((modes, SEGMENTS, LANES), lambda i: (0, 0, i))
    flat = pltpu.VMEM((tokens, LANES), jnp.float32)
    pad = pltpu.VMEM((tokens + HALO, LANES), jnp.float32)
    chunks = channels // LANES
    work = tokens * channels * modes

    segment_ends, local_end = pl.pallas_call(
        ends_kernel,
        grid=(chunks,),
        in_specs=[stream, stream, edges, taps, mode],
        out_specs=[segs, mode],
        out_shape=[
            jax.ShapeDtypeStruct((modes, SEGMENTS, channels), jnp.float32),
            jax.ShapeDtypeStruct((modes, channels), jnp.float32),
        ],
        scratch_shapes=[pad, flat],
        compiler_params=pltpu.CompilerParams(vmem_limit_bytes=32 * MIB),
        cost_estimate=pl.CostEstimate(flops=2 * work, bytes_accessed=4 * tokens * channels, transcendentals=0),
        name="segment_ends",
    )(key_in, value_in, edge, short_filter, rate)

    ends = lax.all_gather(local_end[None], "ctx", axis=0, tiled=True)
    hops = position - 1 - jnp.arange(blocks)
    span = (tokens * jnp.maximum(hops, 0)).astype(jnp.float32)
    weights = jnp.where(
        (hops >= 0)[:, None, None], jnp.exp(-rate[None] * span[:, None, None]), 0.0
    )
    carry = jnp.sum(weights * ends, axis=0)

    gated = pl.pallas_call(
        gated_kernel,
        grid=(chunks,),
        in_specs=[
            stream, stream, stream, edges, taps, mode, mode,
            pl.BlockSpec((1, LANES), lambda i: (0, i)), segs, mode,
        ],
        out_specs=stream,
        out_shape=jax.ShapeDtypeStruct((tokens, channels), jnp.bfloat16),
        scratch_shapes=[pad, flat, flat, flat, pltpu.VMEM((modes, SEGMENTS, LANES), jnp.float32)],
        compiler_params=pltpu.CompilerParams(vmem_limit_bytes=32 * MIB),
        cost_estimate=pl.CostEstimate(flops=4 * work, bytes_accessed=8 * tokens * channels, transcendentals=0),
        name="gated",
    )(query_in, key_in, value_in, edge, short_filter, rate, gain, skip, segment_ends, carry)

    depth, columns = out_weight.shape
    partners = blocks // 2
    return pl.pallas_call(
        functools.partial(mix_kernel, shards, blocks),
        in_specs=[pl.BlockSpec(memory_space=pl.ANY)] * 2,
        out_specs=pl.BlockSpec(memory_space=pltpu.VMEM),
        out_shape=jax.ShapeDtypeStruct((tokens, columns), jnp.bfloat16),
        scratch_shapes=[
            pltpu.VMEM((shards, tokens, channels), jnp.bfloat16),
            pltpu.VMEM((blocks * depth, columns), jnp.bfloat16),
            pltpu.VMEM((tokens, columns), jnp.float32),
            pltpu.SemaphoreType.DMA,
            pltpu.SemaphoreType.DMA,
            pltpu.SemaphoreType.DMA((shards, PIECES, 3)),
            pltpu.SemaphoreType.DMA((shards, PIECES)),
            pltpu.SemaphoreType.DMA((2 * partners,)),
            pltpu.SemaphoreType.DMA((blocks,)),
        ],
        compiler_params=pltpu.CompilerParams(
            collective_id=0, has_side_effects=True, vmem_limit_bytes=60 * MIB
        ),
        cost_estimate=pl.CostEstimate(
            flops=2 * tokens * shards * channels * columns,
            bytes_accessed=2 * tokens * channels + 2 * depth * columns + 2 * tokens * columns,
            transcendentals=0,
        ),
        name="mix",
    )(gated, out_weight)


def solution(mesh):
    in_specs = (
        P("ctx", "chan"),
        P("ctx", "chan"),
        P("ctx", "chan"),
        P(None, None, "chan"),
        P("chan", None),
        P("chan", None),
        P("chan"),
        P("ctx", "chan"),
    )
    return jax.shard_map(
        on_device, mesh=mesh, in_specs=in_specs, out_specs=P("ctx", "chan"), check_vma=False
    )
```

```python
import functools

import jax
import jax.numpy as jnp
from jax import lax
from jax.experimental import pallas as pl
from jax.experimental.pallas import tpu as pltpu
from jax.sharding import PartitionSpec as P

MESH = pl.DeviceIdType.MESH
SEGMENTS = 8
LANES = 128
HALO = 8
PIECES = 4
MIB = 1024 * 1024


def short_stream(x_ref, edge_ref, taps, padded, result_of, length):
    padded[HALO - edge_ref.shape[0] : HALO, :] = edge_ref[...]
    for seg in range(SEGMENTS):
        at = seg * length
        padded[HALO + at : HALO + at + length, :] = x_ref[at : at + length, :].astype(jnp.float32)
    for seg in range(SEGMENTS):
        at = seg * length
        total = None
        for tap in range(taps.shape[0]):
            begin = HALO + at - tap
            term = taps[tap : tap + 1, :] * padded[begin : begin + length, :]
            total = term if total is None else total + term
        result_of(at, total)


def write_to(ref, length):
    def put(at, value):
        ref[at : at + length, :] = value

    return put


def multiply_into(ref, length):
    def put(at, value):
        ref[at : at + length, :] = ref[at : at + length, :] * value

    return put


def ends_kernel(k_ref, v_ref, edge_ref, taps_ref, rate_ref, seg_ref, end_ref, padded, drive):
    tokens = k_ref.shape[0]
    modes = rate_ref.shape[0]
    length = tokens // SEGMENTS
    short_stream(k_ref, edge_ref.at[1], taps_ref.at[1], padded, write_to(drive, length), length)
    short_stream(v_ref, edge_ref.at[2], taps_ref.at[2], padded, multiply_into(drive, length), length)
    decay = jnp.exp(-rate_ref[...])
    decays = [jnp.broadcast_to(decay[n : n + 1, :], (SEGMENTS, LANES)) for n in range(modes)]
    unroll = 4

    def steps(block, states):
        for inner in range(unroll):
            u = drive[pl.ds(block * unroll + inner, SEGMENTS, stride=length), :]
            states = tuple(decays[n] * states[n] + u for n in range(modes))
        return states

    zero = jnp.zeros((SEGMENTS, LANES), jnp.float32)
    states = lax.fori_loop(0, length // unroll, steps, (zero,) * modes)
    for n in range(modes):
        seg_ref[n] = states[n]
    span = jnp.exp(-rate_ref[...] * float(length))
    total = jnp.zeros((modes, LANES), jnp.float32)
    for seg in range(SEGMENTS):
        total = span * total + seg_ref[:, seg, :]
    end_ref[...] = total


def gate_chunk(
    streams, edge_ref, taps_ref, rate, gain, skip, seg_ref, carry,
    out_ref, padded, drive, query, conv, starts,
):
    tokens = drive.shape[0]
    modes = rate.shape[0]
    length = tokens // SEGMENTS
    q_ref, k_ref, v_ref = streams
    short_stream(q_ref, edge_ref.at[0], taps_ref.at[0], padded, write_to(query, length), length)
    short_stream(k_ref, edge_ref.at[1], taps_ref.at[1], padded, write_to(drive, length), length)
    short_stream(v_ref, edge_ref.at[2], taps_ref.at[2], padded, multiply_into(drive, length), length)
    span = jnp.exp(-rate * float(length))
    state = carry
    for seg in range(SEGMENTS):
        starts[:, seg, :] = state
        state = span * state + seg_ref[:, seg, :]
    decay = jnp.exp(-rate)
    decays = [jnp.broadcast_to(decay[n : n + 1, :], (SEGMENTS, LANES)) for n in range(modes)]
    gains = [jnp.broadcast_to(gain[n : n + 1, :], (SEGMENTS, LANES)) for n in range(modes)]
    unroll = 4

    def steps(block, states):
        for inner in range(unroll):
            at = block * unroll + inner
            u = drive[pl.ds(at, SEGMENTS, stride=length), :]
            states = tuple(decays[n] * states[n] + u for n in range(modes))
            even, odd = gains[0] * states[0], gains[1] * states[1]
            for n in range(2, modes, 2):
                even = even + gains[n] * states[n]
                odd = odd + gains[n + 1] * states[n + 1]
            conv[pl.ds(at, SEGMENTS, stride=length), :] = even + odd
        return states

    lax.fori_loop(0, length // unroll, steps, tuple(starts[n] for n in range(modes)))
    for seg in range(SEGMENTS):
        at = seg * length
        rows = slice(at, at + length)
        out_ref[rows, :] = (
            query[rows, :] * (conv[rows, :] + skip * drive[rows, :])
        ).astype(out_ref.dtype)


def route(shards):
    line = shards // 2
    plans = []
    for me in range(shards):
        z, y = me // 2, me % 2
        events = []
        for shard in range(shards):
            from_z, from_y = shard // 2, shard % 2
            apart = abs(from_z - z)
            halves = []
            for half in range(2):
                if from_y == y:
                    low = z > 0 and from_z >= z
                    high = z < line - 1 and from_z <= z
                    pair = not (half == 1 and apart == 1)
                    key = float(apart)
                else:
                    low = z > 0 and apart == 0 and half == 1
                    high = z < line - 1 and apart == 0 and half == 1
                    pair = False
                    key = apart + 0.5
                halves.append((low, high, pair))
            events.append((key, shard, halves))
        events.sort(key=lambda e: (e[0], e[1]))
        plans.append([
            (shard, [int(a) + 2 * int(b) + 4 * int(c) for a, b, c in halves])
            for _, shard, halves in events
        ])
    return plans


def pick(values, index):
    result = jnp.int32(values[0])
    for position in range(1, len(values)):
        result = jnp.where(index == position, values[position], result)
    return result


def mix_kernel(
    shards, blocks, q_ref, k_ref, v_ref, w_ref, edge_ref, taps_ref, rate_ref, gain_ref, skip_ref,
    seg_ref, carry_ref, out_ref, held, weight, total, streams, padded, drive, query, conv, starts,
    in_sem, wown_sem, send_sem, recv_sem, wsend_sem, wrecv_sem,
):
    tokens, channels = q_ref.shape
    depth, columns = w_ref.shape
    width = channels // PIECES
    chunks = channels // LANES
    per_piece = width // LANES
    me = lax.axis_index("chan")
    ctx = lax.axis_index("ctx")
    line = shards // 2
    z, y = me // 2, me % 2
    plans = route(shards)
    codes = [
        pick([plan[k][0] + shards * (plan[k][1][0] + 8 * plan[k][1][1]) for plan in plans], me)
        for k in range(shards)
    ]
    targets = (me - 2, me + 2, me + 1 - 2 * y)

    def flip(by):
        result, bit = ctx, 1
        while bit <= by:
            if by & bit:
                result = result + bit * (1 - 2 * ((ctx // bit) % 2))
            bit *= 2
        return result

    def block_of(index):
        return weight.at[pl.ds(pl.multiple_of(index * depth, depth), depth), :]

    def fetch(chunk, act):
        slot = chunk % 2
        lanes = pl.ds(pl.multiple_of(chunk * LANES, LANES), LANES)
        for which, ref in enumerate((q_ref, k_ref, v_ref)):
            act(
                pltpu.make_async_copy(
                    ref.at[:, lanes], streams.at[slot, which], in_sem.at[slot, which]
                )
            )

    fetch(0, lambda copy: copy.start())
    weight_copy = pltpu.make_async_copy(w_ref, block_of(ctx), wown_sem)
    weight_copy.start()

    barrier = pltpu.get_barrier_semaphore()

    @pl.when(z > 0)
    def _():
        pl.semaphore_signal(barrier, inc=1, device_id={"chan": targets[0]}, device_id_type=MESH)

    @pl.when(z < line - 1)
    def _():
        pl.semaphore_signal(barrier, inc=1, device_id={"chan": targets[1]}, device_id_type=MESH)

    pl.semaphore_signal(barrier, inc=1, device_id={"chan": targets[2]}, device_id_type=MESH)
    partners = [1] + list(range(2, blocks, 2))
    for by in partners:
        pl.semaphore_signal(barrier, inc=1, device_id={"ctx": flip(by)}, device_id_type=MESH)
    lines = jnp.where(z > 0, 1, 0) + jnp.where(z < line - 1, 1, 0)
    pl.semaphore_wait(barrier, lines + 1 + len(partners))

    def piece_copy(shard, piece, way):
        part = held.at[shard, piece]
        return pltpu.make_async_remote_copy(
            src_ref=part,
            dst_ref=part,
            send_sem=send_sem.at[shard, piece, way],
            recv_sem=recv_sem.at[shard, piece],
            device_id={"chan": targets[way]},
            device_id_type=MESH,
        )

    def weight_send(block, by, slot):
        return pltpu.make_async_remote_copy(
            src_ref=block_of(block),
            dst_ref=block_of(block),
            send_sem=wsend_sem.at[slot],
            recv_sem=wrecv_sem.at[block],
            device_id={"ctx": flip(by)},
            device_id_type=MESH,
        )

    def onward(code, piece, act):
        shard = code % shards
        flags = code // shards
        flags = jnp.where(piece < PIECES // 2, flags % 8, flags // 8)
        for way, bit in ((0, flags % 2), (1, (flags // 2) % 2), (2, flags // 4)):

            @pl.when(bit == 1)
            def _(way=way):
                act(piece_copy(shard, piece, way))

    weight_copy.wait()
    first_sends = [weight_send(ctx, by, slot) for slot, by in enumerate(partners)]
    for copy in first_sends:
        copy.start()

    @pl.loop(0, chunks)
    def _(chunk):
        @pl.when(chunk < chunks - 1)
        def _():
            fetch(chunk + 1, lambda copy: copy.start())

        fetch(chunk, lambda copy: copy.wait())
        piece = chunk // per_piece
        lanes = pl.ds(pl.multiple_of(chunk * LANES, LANES), LANES)
        inside = pl.ds(pl.multiple_of((chunk % per_piece) * LANES, LANES), LANES)
        gate_chunk(
            [streams.at[chunk % 2, which] for which in range(3)],
            edge_ref.at[:, :, lanes],
            taps_ref.at[:, :, lanes],
            rate_ref[:, lanes],
            gain_ref[:, lanes],
            skip_ref[:, lanes],
            seg_ref.at[:, :, lanes],
            carry_ref[:, lanes],
            held.at[me, piece, :, inside],
            padded, drive, query, conv, starts,
        )

        @pl.when(chunk % per_piece == per_piece - 1)
        def _():
            onward(codes[0], piece, lambda copy: copy.start())

    def zero_rows(at):
        total[pl.ds(pl.multiple_of(at * 64, 64), 64), :] = jnp.zeros((64, columns), jnp.float32)

    pl.loop(0, tokens // 64)(zero_rows)

    def arrive(code, piece):
        piece_copy(code % shards, piece, 2).wait_recv()
        onward(code, piece, lambda copy: copy.start())

    half = shards // 2
    later_sends = []
    for k in range(1, half):
        code = codes[k]
        if k < half - 1:

            @pl.loop(0, PIECES)
            def _(piece, code=code):
                arrive(code, piece)
        else:

            @pl.loop(0, PIECES // 2)
            def _(piece, code=code):
                arrive(code, piece)

            for by in partners[1:]:
                block = flip(by)
                weight_send(block, 1, 0).wait_recv()
                copy = weight_send(block, 1, len(partners) + len(later_sends))
                copy.start()
                later_sends.append(copy)

            @pl.loop(PIECES // 2, PIECES)
            def _(piece, code=code):
                arrive(code, piece)

    weight_send(flip(1), 1, 0).wait_recv()
    for by in partners[1:]:
        weight_send(flip(by + 1), 1, 0).wait_recv()

    tile = 256

    rows = tokens // 2

    def multiply(shard, piece):
        deep = pl.ds(pl.multiple_of(shard * channels + piece * width, width), width)

        @pl.loop(0, columns // tile)
        def _(part):
            cols = pl.ds(pl.multiple_of(part * tile, tile), tile)
            for at in range(0, tokens, rows):
                total[at : at + rows, cols] += jnp.dot(
                    held[shard, piece, at : at + rows, :],
                    weight[deep, cols],
                    preferred_element_type=jnp.float32,
                )

    @pl.loop(half, shards)
    def _(k):
        code = pick(codes, k)
        earlier = pick(codes, 2 * (k - half)) % shards
        later = pick(codes, 2 * (k - half) + 1) % shards

        @pl.loop(0, PIECES)
        def _(piece):
            arrive(code, piece)
            multiply(earlier, piece)
            multiply(later, piece)

    def round_rows(at):
        here = pl.ds(pl.multiple_of(at * 64, 64), 64)
        out_ref[here, :] = total[here, :].astype(out_ref.dtype)

    pl.loop(0, tokens // 64)(round_rows)

    @pl.loop(0, shards)
    def _(k):
        code = pick(codes, k)

        @pl.loop(0, PIECES)
        def _(piece):
            onward(code, piece, lambda copy: copy.wait_send())

    for copy in first_sends + later_sends:
        copy.wait_send()


def on_device(query_in, key_in, value_in, short_filter, residue, decay_rate, skip_gain, out_weight):
    tokens, channels = query_in.shape
    tap_count = short_filter.shape[1]
    modes = decay_rate.shape[1]
    shards = lax.axis_size("chan")
    blocks = lax.axis_size("ctx")
    position = lax.axis_index("ctx")
    edge = jnp.stack([x[tokens - (tap_count - 1) :, :] for x in (query_in, key_in, value_in)])
    edge = lax.ppermute(edge, "ctx", [(i, i + 1) for i in range(blocks - 1)])
    edge = edge.astype(jnp.float32)
    rate = decay_rate.T
    gain = (residue * jnp.sqrt(decay_rate)).T
    skip = skip_gain[None, :]

    stream = pl.BlockSpec((tokens, LANES), lambda i: (0, i))
    edges = pl.BlockSpec((3, tap_count - 1, LANES), lambda i: (0, 0, i))
    taps = pl.BlockSpec((3, tap_count, LANES), lambda i: (0, 0, i))
    mode = pl.BlockSpec((modes, LANES), lambda i: (0, i))
    segs = pl.BlockSpec((modes, SEGMENTS, LANES), lambda i: (0, 0, i))
    flat = pltpu.VMEM((tokens, LANES), jnp.float32)
    pad = pltpu.VMEM((tokens + HALO, LANES), jnp.float32)
    chunks = channels // LANES
    work = tokens * channels * modes

    segment_ends, local_end = pl.pallas_call(
        ends_kernel,
        grid=(chunks,),
        in_specs=[stream, stream, edges, taps, mode],
        out_specs=[segs, mode],
        out_shape=[
            jax.ShapeDtypeStruct((modes, SEGMENTS, channels), jnp.float32),
            jax.ShapeDtypeStruct((modes, channels), jnp.float32),
        ],
        scratch_shapes=[pad, flat],
        compiler_params=pltpu.CompilerParams(vmem_limit_bytes=32 * MIB),
        cost_estimate=pl.CostEstimate(flops=2 * work, bytes_accessed=4 * tokens * channels, transcendentals=0),
        name="segment_ends",
    )(key_in, value_in, edge, short_filter, rate)

    ends = lax.all_gather(local_end[None], "ctx", axis=0, tiled=True)
    hops = position - 1 - jnp.arange(blocks)
    span = (tokens * jnp.maximum(hops, 0)).astype(jnp.float32)
    weights = jnp.where(
        (hops >= 0)[:, None, None], jnp.exp(-rate[None] * span[:, None, None]), 0.0
    )
    carry = jnp.sum(weights * ends, axis=0)

    depth, columns = out_weight.shape
    partners = blocks // 2
    return pl.pallas_call(
        functools.partial(mix_kernel, shards, blocks),
        in_specs=[pl.BlockSpec(memory_space=pl.ANY)] * 4
        + [pl.BlockSpec(memory_space=pltpu.VMEM)] * 7,
        out_specs=pl.BlockSpec(memory_space=pltpu.VMEM),
        out_shape=jax.ShapeDtypeStruct((tokens, columns), jnp.bfloat16),
        scratch_shapes=[
            pltpu.VMEM((shards, PIECES, tokens, channels // PIECES), jnp.bfloat16),
            pltpu.VMEM((blocks * depth, columns), jnp.bfloat16),
            pltpu.VMEM((tokens, columns), jnp.float32),
            pltpu.VMEM((2, 3, tokens, LANES), jnp.bfloat16),
            pad,
            flat,
            flat,
            flat,
            pltpu.VMEM((modes, SEGMENTS, LANES), jnp.float32),
            pltpu.SemaphoreType.DMA((2, 3)),
            pltpu.SemaphoreType.DMA,
            pltpu.SemaphoreType.DMA((shards, PIECES, 3)),
            pltpu.SemaphoreType.DMA((shards, PIECES)),
            pltpu.SemaphoreType.DMA((2 * partners,)),
            pltpu.SemaphoreType.DMA((blocks,)),
        ],
        compiler_params=pltpu.CompilerParams(
            collective_id=0, has_side_effects=True, vmem_limit_bytes=62 * MIB
        ),
        cost_estimate=pl.CostEstimate(
            flops=2 * tokens * shards * channels * columns + 4 * work,
            bytes_accessed=6 * tokens * channels + 2 * depth * columns + 2 * tokens * columns,
            transcendentals=0,
        ),
        name="mix",
    )(
        query_in, key_in, value_in, out_weight, edge, short_filter, rate, gain, skip,
        segment_ends, carry,
    )


def solution(mesh):
    in_specs = (
        P("ctx", "chan"),
        P("ctx", "chan"),
        P("ctx", "chan"),
        P(None, None, "chan"),
        P("chan", None),
        P("chan", None),
        P("chan"),
        P("ctx", "chan"),
    )
    return jax.shard_map(
        on_device, mesh=mesh, in_specs=in_specs, out_specs=P("ctx", "chan"), check_vma=False
    )
```

```python
import functools

import jax
import jax.numpy as jnp
from jax import lax
from jax.experimental import pallas as pl
from jax.experimental.pallas import tpu as pltpu
from jax.sharding import PartitionSpec as P

MESH = pl.DeviceIdType.MESH
SEGMENTS = 8
LANES = 128
HALO = 8
PIECES = 4
MIB = 1024 * 1024


def short_stream(x_ref, edge_ref, taps, padded, result_of, length):
    padded[HALO - edge_ref.shape[0] : HALO, :] = edge_ref[...]
    for seg in range(SEGMENTS):
        at = seg * length
        padded[HALO + at : HALO + at + length, :] = x_ref[at : at + length, :].astype(jnp.float32)
    for seg in range(SEGMENTS):
        at = seg * length
        total = None
        for tap in range(taps.shape[0]):
            begin = HALO + at - tap
            term = taps[tap : tap + 1, :] * padded[begin : begin + length, :]
            total = term if total is None else total + term
        result_of(at, total)


def write_to(ref, length):
    def put(at, value):
        ref[at : at + length, :] = value

    return put


def multiply_into(ref, length):
    def put(at, value):
        ref[at : at + length, :] = ref[at : at + length, :] * value

    return put


def end_chunk(streams, edge_ref, taps_ref, rate, kept, seg_ref, end_ref, padded, drive):
    tokens = drive.shape[0]
    modes = rate.shape[0]
    length = tokens // SEGMENTS
    k_ref, v_ref = streams
    short_stream(k_ref, edge_ref.at[1], taps_ref.at[1], padded, write_to(drive, length), length)
    short_stream(v_ref, edge_ref.at[2], taps_ref.at[2], padded, multiply_into(drive, length), length)
    decay = jnp.exp(-rate)
    decays = [jnp.broadcast_to(decay[n : n + 1, :], (SEGMENTS, LANES)) for n in range(modes)]
    unroll = 4

    def steps(block, states):
        for inner in range(unroll):
            u = drive[pl.ds(block * unroll + inner, SEGMENTS, stride=length), :]
            states = tuple(decays[n] * states[n] + u for n in range(modes))
        return states

    zero = jnp.zeros((SEGMENTS, LANES), jnp.float32)
    states = lax.fori_loop(0, length // unroll, steps, (zero,) * modes)
    for n in range(modes):
        seg_ref[n] = states[n]
    span = jnp.exp(-rate * float(length))
    total = jnp.zeros((modes, LANES), jnp.float32)
    for seg in range(SEGMENTS):
        total = span * total + seg_ref[:, seg, :]
        rows = slice(seg * length, (seg + 1) * length)
        kept[rows, :] = drive[rows, :]
    end_ref[...] = total


def gate_chunk(
    q_ref, edge_ref, taps_ref, rate, gain, skip, seg_ref, carry, kept,
    out_ref, padded, drive, query, conv, starts,
):
    tokens = drive.shape[0]
    modes = rate.shape[0]
    length = tokens // SEGMENTS
    short_stream(q_ref, edge_ref.at[0], taps_ref.at[0], padded, write_to(query, length), length)
    span = jnp.exp(-rate * float(length))
    state = carry
    for seg in range(SEGMENTS):
        starts[:, seg, :] = state
        state = span * state + seg_ref[:, seg, :]
        rows = slice(seg * length, (seg + 1) * length)
        drive[rows, :] = kept[rows, :]
    decay = jnp.exp(-rate)
    decays = [jnp.broadcast_to(decay[n : n + 1, :], (SEGMENTS, LANES)) for n in range(modes)]
    gains = [jnp.broadcast_to(gain[n : n + 1, :], (SEGMENTS, LANES)) for n in range(modes)]
    unroll = 4

    def steps(block, states):
        for inner in range(unroll):
            at = block * unroll + inner
            u = drive[pl.ds(at, SEGMENTS, stride=length), :]
            states = tuple(decays[n] * states[n] + u for n in range(modes))
            even, odd = gains[0] * states[0], gains[1] * states[1]
            for n in range(2, modes, 2):
                even = even + gains[n] * states[n]
                odd = odd + gains[n + 1] * states[n + 1]
            conv[pl.ds(at, SEGMENTS, stride=length), :] = even + odd
        return states

    lax.fori_loop(0, length // unroll, steps, tuple(starts[n] for n in range(modes)))
    for seg in range(SEGMENTS):
        at = seg * length
        rows = slice(at, at + length)
        out_ref[rows, :] = (
            query[rows, :] * (conv[rows, :] + skip * drive[rows, :])
        ).astype(out_ref.dtype)


def route(shards):
    line = shards // 2
    plans = []
    for me in range(shards):
        z, y = me // 2, me % 2
        events = []
        for shard in range(shards):
            from_z, from_y = shard // 2, shard % 2
            apart = abs(from_z - z)
            halves = []
            for half in range(2):
                if from_y == y:
                    low = z > 0 and from_z >= z
                    high = z < line - 1 and from_z <= z
                    pair = not (half == 1 and apart == 1)
                    key = float(apart)
                else:
                    low = z > 0 and apart == 0 and half == 1
                    high = z < line - 1 and apart == 0 and half == 1
                    pair = False
                    key = apart + 0.5
                halves.append((low, high, pair))
            events.append((key, shard, halves))
        events.sort(key=lambda e: (e[0], e[1]))
        plans.append([
            (shard, [int(a) + 2 * int(b) + 4 * int(c) for a, b, c in halves])
            for _, shard, halves in events
        ])
    return plans


def pick(values, index):
    result = jnp.int32(values[0])
    for position in range(1, len(values)):
        result = jnp.where(index == position, values[position], result)
    return result


def mix_kernel(
    shards, blocks, q_ref, k_ref, v_ref, w_ref, edge_ref, taps_ref, rate_ref, gain_ref, skip_ref,
    out_ref, held, weight, total, streams, padded, drive, query, conv, starts, segs, ends,
    in_sem, esend_sem, erecv_sem, wown_sem, send_sem, recv_sem, wsend_sem, wrecv_sem,
):
    tokens, channels = q_ref.shape
    depth, columns = w_ref.shape
    width = channels // PIECES
    chunks = channels // LANES
    per_piece = width // LANES
    me = lax.axis_index("chan")
    ctx = lax.axis_index("ctx")
    line = shards // 2
    z, y = me // 2, me % 2
    plans = route(shards)
    codes = [
        pick([plan[k][0] + shards * (plan[k][1][0] + 8 * plan[k][1][1]) for plan in plans], me)
        for k in range(shards)
    ]
    targets = (me - 2, me + 2, me + 1 - 2 * y)

    def flip(by):
        result, bit = ctx, 1
        while bit <= by:
            if by & bit:
                result = result + bit * (1 - 2 * ((ctx // bit) % 2))
            bit *= 2
        return result

    def block_of(index):
        return weight.at[pl.ds(pl.multiple_of(index * depth, depth), depth), :]

    def fetch(chunk, names, act):
        slot = chunk % 2
        lanes = pl.ds(pl.multiple_of(chunk * LANES, LANES), LANES)
        for which in names:
            act(
                pltpu.make_async_copy(
                    (q_ref, k_ref, v_ref)[which].at[:, lanes],
                    streams.at[slot, which],
                    in_sem.at[slot, which],
                )
            )

    fetch(0, (0, 1, 2), lambda copy: copy.start())
    weight_copy = pltpu.make_async_copy(w_ref, block_of(ctx), wown_sem)
    weight_copy.start()

    barrier = pltpu.get_barrier_semaphore()

    @pl.when(z > 0)
    def _():
        pl.semaphore_signal(barrier, inc=1, device_id={"chan": targets[0]}, device_id_type=MESH)

    @pl.when(z < line - 1)
    def _():
        pl.semaphore_signal(barrier, inc=1, device_id={"chan": targets[1]}, device_id_type=MESH)

    pl.semaphore_signal(barrier, inc=1, device_id={"chan": targets[2]}, device_id_type=MESH)
    partners = [1] + list(range(2, blocks, 2))
    for by in range(1, blocks):
        pl.semaphore_signal(barrier, inc=1, device_id={"ctx": flip(by)}, device_id_type=MESH)
    lines = jnp.where(z > 0, 1, 0) + jnp.where(z < line - 1, 1, 0)
    pl.semaphore_wait(barrier, lines + blocks)

    def piece_copy(shard, piece, way):
        part = held.at[shard, piece]
        return pltpu.make_async_remote_copy(
            src_ref=part,
            dst_ref=part,
            send_sem=send_sem.at[shard, piece, way],
            recv_sem=recv_sem.at[shard, piece],
            device_id={"chan": targets[way]},
            device_id_type=MESH,
        )

    def weight_send(block, by, slot):
        return pltpu.make_async_remote_copy(
            src_ref=block_of(block),
            dst_ref=block_of(block),
            send_sem=wsend_sem.at[slot],
            recv_sem=wrecv_sem.at[block],
            device_id={"ctx": flip(by)},
            device_id_type=MESH,
        )

    def onward(code, piece, act):
        shard = code % shards
        flags = code // shards
        flags = jnp.where(piece < PIECES // 2, flags % 8, flags // 8)
        for way, bit in ((0, flags % 2), (1, (flags // 2) % 2), (2, flags // 4)):

            @pl.when(bit == 1)
            def _(way=way):
                act(piece_copy(shard, piece, way))

    weight_copy.wait()
    first_sends = [weight_send(ctx, by, slot) for slot, by in enumerate(partners)]
    for copy in first_sends:
        copy.start()

    def ends_copy(source, piece, by):
        part = ends.at[source, piece]
        return pltpu.make_async_remote_copy(
            src_ref=part,
            dst_ref=part,
            send_sem=esend_sem.at[piece, by],
            recv_sem=erecv_sem.at[source, piece],
            device_id={"ctx": flip(by)},
            device_id_type=MESH,
        )

    def places(piece, sub):
        chunk = piece * per_piece + sub
        lanes = pl.ds(pl.multiple_of(chunk * LANES, LANES), LANES)
        inside = pl.ds(pl.multiple_of(sub * LANES, LANES), LANES)
        return chunk, lanes, inside

    def advance(chunk, names):
        @pl.when(chunk < chunks - 1)
        def _():
            fetch(chunk + 1, names, lambda copy: copy.start())

        fetch(chunk, names, lambda copy: copy.wait())

    def end_piece(piece):
        @pl.loop(0, per_piece)
        def _(sub):
            chunk, lanes, inside = places(piece, sub)
            advance(chunk, (1, 2))
            end_chunk(
                [streams.at[chunk % 2, 1], streams.at[chunk % 2, 2]],
                edge_ref.at[:, :, lanes],
                taps_ref.at[:, :, lanes],
                rate_ref[:, lanes],
                total.at[:, lanes],
                segs.at[:, :, lanes],
                ends.at[ctx, piece, :, inside],
                padded, drive,
            )

        for by in range(1, blocks):
            ends_copy(ctx, piece, by).start()

    def gate_piece(piece):
        for by in range(1, blocks):
            ends_copy(flip(by), piece, by).wait_recv()

        @pl.loop(0, per_piece)
        def _(sub):
            chunk, lanes, inside = places(piece, sub)
            advance(chunk, (0,))
            rate = rate_ref[:, lanes]
            carry = jnp.zeros(rate.shape, jnp.float32)
            for source in range(blocks):
                hops = ctx - 1 - source
                span = (tokens * jnp.maximum(hops, 0)).astype(jnp.float32)
                part = jnp.exp(-rate * span) * ends[source, piece, :, inside]
                carry = carry + jnp.where(hops >= 0, part, 0.0)
            gate_chunk(
                streams.at[chunk % 2, 0],
                edge_ref.at[:, :, lanes],
                taps_ref.at[:, :, lanes],
                rate,
                gain_ref[:, lanes],
                skip_ref[:, lanes],
                segs.at[:, :, lanes],
                carry,
                total.at[:, lanes],
                held.at[me, piece, :, inside],
                padded, drive, query, conv, starts,
            )

        onward(codes[0], piece, lambda copy: copy.start())

    @pl.loop(0, PIECES + 1)
    def _(step):
        @pl.when(step < PIECES)
        def _():
            end_piece(step)

        @pl.when(step >= 1)
        def _():
            gate_piece(step - 1)

    def zero_rows(at):
        total[pl.ds(pl.multiple_of(at * 64, 64), 64), :] = jnp.zeros((64, columns), jnp.float32)

    pl.loop(0, tokens // 64)(zero_rows)

    def arrive(code, piece):
        piece_copy(code % shards, piece, 2).wait_recv()
        onward(code, piece, lambda copy: copy.start())

    half = shards // 2
    later_sends = []
    for k in range(1, half):
        code = codes[k]
        if k < half - 1:

            @pl.loop(0, PIECES)
            def _(piece, code=code):
                arrive(code, piece)
        else:

            @pl.loop(0, PIECES // 2)
            def _(piece, code=code):
                arrive(code, piece)

            for by in partners[1:]:
                block = flip(by)
                weight_send(block, 1, 0).wait_recv()
                copy = weight_send(block, 1, len(partners) + len(later_sends))
                copy.start()
                later_sends.append(copy)

            @pl.loop(PIECES // 2, PIECES)
            def _(piece, code=code):
                arrive(code, piece)

    weight_send(flip(1), 1, 0).wait_recv()
    for by in partners[1:]:
        weight_send(flip(by + 1), 1, 0).wait_recv()

    tile = 256

    rows = tokens // 2

    def multiply(shard, piece):
        deep = pl.ds(pl.multiple_of(shard * channels + piece * width, width), width)

        @pl.loop(0, columns // tile)
        def _(part):
            cols = pl.ds(pl.multiple_of(part * tile, tile), tile)
            for at in range(0, tokens, rows):
                total[at : at + rows, cols] += jnp.dot(
                    held[shard, piece, at : at + rows, :],
                    weight[deep, cols],
                    preferred_element_type=jnp.float32,
                )

    @pl.loop(half, shards)
    def _(k):
        code = pick(codes, k)
        earlier = pick(codes, 2 * (k - half)) % shards
        later = pick(codes, 2 * (k - half) + 1) % shards

        @pl.loop(0, PIECES)
        def _(piece):
            arrive(code, piece)
            multiply(earlier, piece)
            multiply(later, piece)

    def round_rows(at):
        here = pl.ds(pl.multiple_of(at * 64, 64), 64)
        out_ref[here, :] = total[here, :].astype(out_ref.dtype)

    pl.loop(0, tokens // 64)(round_rows)

    @pl.loop(0, shards)
    def _(k):
        code = pick(codes, k)

        @pl.loop(0, PIECES)
        def _(piece):
            onward(code, piece, lambda copy: copy.wait_send())

    for copy in first_sends + later_sends:
        copy.wait_send()
    for piece in range(PIECES):
        for by in range(1, blocks):
            ends_copy(ctx, piece, by).wait_send()


def on_device(query_in, key_in, value_in, short_filter, residue, decay_rate, skip_gain, out_weight):
    tokens, channels = query_in.shape
    tap_count = short_filter.shape[1]
    modes = decay_rate.shape[1]
    shards = lax.axis_size("chan")
    blocks = lax.axis_size("ctx")
    edge = jnp.stack([x[tokens - (tap_count - 1) :, :] for x in (query_in, key_in, value_in)])
    edge = lax.ppermute(edge, "ctx", [(i, i + 1) for i in range(blocks - 1)])
    edge = edge.astype(jnp.float32)
    rate = decay_rate.T
    gain = (residue * jnp.sqrt(decay_rate)).T
    skip = skip_gain[None, :]

    flat = pltpu.VMEM((tokens, LANES), jnp.float32)
    pad = pltpu.VMEM((tokens + HALO, LANES), jnp.float32)
    work = tokens * channels * modes
    depth, columns = out_weight.shape
    partners = blocks // 2
    return pl.pallas_call(
        functools.partial(mix_kernel, shards, blocks),
        in_specs=[pl.BlockSpec(memory_space=pl.ANY)] * 4
        + [pl.BlockSpec(memory_space=pltpu.VMEM)] * 5,
        out_specs=pl.BlockSpec(memory_space=pltpu.VMEM),
        out_shape=jax.ShapeDtypeStruct((tokens, columns), jnp.bfloat16),
        scratch_shapes=[
            pltpu.VMEM((shards, PIECES, tokens, channels // PIECES), jnp.bfloat16),
            pltpu.VMEM((blocks * depth, columns), jnp.bfloat16),
            pltpu.VMEM((tokens, columns), jnp.float32),
            pltpu.VMEM((2, 3, tokens, LANES), jnp.bfloat16),
            pad,
            flat,
            flat,
            flat,
            pltpu.VMEM((modes, SEGMENTS, LANES), jnp.float32),
            pltpu.VMEM((modes, SEGMENTS, channels), jnp.float32),
            pltpu.VMEM((blocks, PIECES, modes, channels // PIECES), jnp.float32),
            pltpu.SemaphoreType.DMA((2, 3)),
            pltpu.SemaphoreType.DMA((PIECES, blocks)),
            pltpu.SemaphoreType.DMA((blocks, PIECES)),
            pltpu.SemaphoreType.DMA,
            pltpu.SemaphoreType.DMA((shards, PIECES, 3)),
            pltpu.SemaphoreType.DMA((shards, PIECES)),
            pltpu.SemaphoreType.DMA((2 * partners,)),
            pltpu.SemaphoreType.DMA((blocks,)),
        ],
        compiler_params=pltpu.CompilerParams(
            collective_id=0, has_side_effects=True, vmem_limit_bytes=62 * MIB
        ),
        cost_estimate=pl.CostEstimate(
            flops=2 * tokens * shards * channels * columns + 6 * work,
            bytes_accessed=6 * tokens * channels + 2 * depth * columns + 2 * tokens * columns,
            transcendentals=0,
        ),
        name="mix",
    )(
        query_in, key_in, value_in, out_weight, edge, short_filter, rate, gain, skip,
    )


def solution(mesh):
    in_specs = (
        P("ctx", "chan"),
        P("ctx", "chan"),
        P("ctx", "chan"),
        P(None, None, "chan"),
        P("chan", None),
        P("chan", None),
        P("chan"),
        P("ctx", "chan"),
    )
    return jax.shard_map(
        on_device, mesh=mesh, in_specs=in_specs, out_specs=P("ctx", "chan"), check_vma=False
    )
```

```python
import functools

import jax
import jax.numpy as jnp
from jax import lax
from jax.experimental import pallas as pl
from jax.experimental.pallas import tpu as pltpu
from jax.sharding import PartitionSpec as P

MESH = pl.DeviceIdType.MESH
SEGMENTS = 8
LANES = 128
HALO = 8
PIECES = 4
MIB = 1024 * 1024


def short_stream(x_ref, edge_ref, taps, padded, result_of, length):
    padded[HALO - edge_ref.shape[0] : HALO, :] = edge_ref[...]
    for seg in range(SEGMENTS):
        at = seg * length
        padded[HALO + at : HALO + at + length, :] = x_ref[at : at + length, :].astype(jnp.float32)
    for seg in range(SEGMENTS):
        at = seg * length
        total = None
        for tap in range(taps.shape[0]):
            begin = HALO + at - tap
            term = taps[tap : tap + 1, :] * padded[begin : begin + length, :]
            total = term if total is None else total + term
        result_of(at, total)


def write_to(ref, length):
    def put(at, value):
        ref[at : at + length, :] = value

    return put


def multiply_into(ref, length):
    def put(at, value):
        ref[at : at + length, :] = ref[at : at + length, :] * value

    return put


def end_chunk(streams, edge_ref, taps_ref, rate, kept, seg_ref, end_ref, padded, drive):
    tokens = drive.shape[0]
    modes = rate.shape[0]
    length = tokens // SEGMENTS
    k_ref, v_ref = streams
    short_stream(k_ref, edge_ref.at[1], taps_ref.at[1], padded, write_to(drive, length), length)
    short_stream(v_ref, edge_ref.at[2], taps_ref.at[2], padded, multiply_into(drive, length), length)
    decay = jnp.exp(-rate)
    decays = [jnp.broadcast_to(decay[n : n + 1, :], (SEGMENTS, LANES)) for n in range(modes)]
    unroll = 4

    def steps(block, states):
        for inner in range(unroll):
            u = drive[pl.ds(block * unroll + inner, SEGMENTS, stride=length), :]
            states = tuple(decays[n] * states[n] + u for n in range(modes))
        return states

    zero = jnp.zeros((SEGMENTS, LANES), jnp.float32)
    states = lax.fori_loop(0, length // unroll, steps, (zero,) * modes)
    for n in range(modes):
        seg_ref[n] = states[n]
    span = jnp.exp(-rate * float(length))
    total = jnp.zeros((modes, LANES), jnp.float32)
    for seg in range(SEGMENTS):
        total = span * total + seg_ref[:, seg, :]
        rows = slice(seg * length, (seg + 1) * length)
        kept[rows, :] = drive[rows, :]
    end_ref[...] = total


def gate_chunk(
    q_ref, edge_ref, taps_ref, rate, gain, skip, seg_ref, carry, kept,
    out_ref, padded, drive, query, conv, starts,
):
    tokens = drive.shape[0]
    modes = rate.shape[0]
    length = tokens // SEGMENTS
    short_stream(q_ref, edge_ref.at[0], taps_ref.at[0], padded, write_to(query, length), length)
    span = jnp.exp(-rate * float(length))
    state = carry
    for seg in range(SEGMENTS):
        starts[:, seg, :] = state
        state = span * state + seg_ref[:, seg, :]
        rows = slice(seg * length, (seg + 1) * length)
        drive[rows, :] = kept[rows, :]
    decay = jnp.exp(-rate)
    decays = [jnp.broadcast_to(decay[n : n + 1, :], (SEGMENTS, LANES)) for n in range(modes)]
    gains = [jnp.broadcast_to(gain[n : n + 1, :], (SEGMENTS, LANES)) for n in range(modes)]
    unroll = 4

    def steps(block, states):
        for inner in range(unroll):
            at = block * unroll + inner
            u = drive[pl.ds(at, SEGMENTS, stride=length), :]
            states = tuple(decays[n] * states[n] + u for n in range(modes))
            even, odd = gains[0] * states[0], gains[1] * states[1]
            for n in range(2, modes, 2):
                even = even + gains[n] * states[n]
                odd = odd + gains[n + 1] * states[n + 1]
            conv[pl.ds(at, SEGMENTS, stride=length), :] = even + odd
        return states

    lax.fori_loop(0, length // unroll, steps, tuple(starts[n] for n in range(modes)))
    for seg in range(SEGMENTS):
        at = seg * length
        rows = slice(at, at + length)
        out_ref[rows, :] = (
            query[rows, :] * (conv[rows, :] + skip * drive[rows, :])
        ).astype(out_ref.dtype)


def route(shards):
    line = shards // 2
    plans = []
    for me in range(shards):
        z, y = me // 2, me % 2
        events = []
        for shard in range(shards):
            from_z, from_y = shard // 2, shard % 2
            apart = abs(from_z - z)
            halves = []
            for half in range(2):
                if from_y == y:
                    low = z > 0 and from_z >= z
                    high = z < line - 1 and from_z <= z
                    pair = not (half == 1 and apart == 1)
                    key = float(apart)
                else:
                    low = z > 0 and apart == 0 and half == 1
                    high = z < line - 1 and apart == 0 and half == 1
                    pair = False
                    key = apart + 0.5
                halves.append((low, high, pair))
            events.append((key, shard, halves))
        events.sort(key=lambda e: (e[0], e[1]))
        plans.append([
            (shard, [int(a) + 2 * int(b) + 4 * int(c) for a, b, c in halves])
            for _, shard, halves in events
        ])
    return plans


def pick(values, index):
    result = jnp.int32(values[0])
    for position in range(1, len(values)):
        result = jnp.where(index == position, values[position], result)
    return result


def mix_kernel(
    shards, blocks, q_ref, k_ref, v_ref, w_ref, edge_ref, taps_ref, rate_ref, gain_ref, skip_ref,
    out_ref, held, weight, total, streams, padded, drive, query, conv, starts, segs, ends,
    in_sem, esend_sem, erecv_sem, wown_sem, send_sem, recv_sem, wsend_sem, wrecv_sem,
):
    tokens, channels = q_ref.shape
    depth, columns = w_ref.shape
    width = channels // PIECES
    chunks = channels // LANES
    per_piece = width // LANES
    me = lax.axis_index("chan")
    ctx = lax.axis_index("ctx")
    line = shards // 2
    z, y = me // 2, me % 2
    plans = route(shards)
    codes = [
        pick([plan[k][0] + shards * (plan[k][1][0] + 8 * plan[k][1][1]) for plan in plans], me)
        for k in range(shards)
    ]
    targets = (me - 2, me + 2, me + 1 - 2 * y)

    def flip(by):
        result, bit = ctx, 1
        while bit <= by:
            if by & bit:
                result = result + bit * (1 - 2 * ((ctx // bit) % 2))
            bit *= 2
        return result

    def block_of(index):
        return weight.at[pl.ds(pl.multiple_of(index * depth, depth), depth), :]

    def fetch(chunk, names, act):
        slot = chunk % 2
        lanes = pl.ds(pl.multiple_of(chunk * LANES, LANES), LANES)
        for which in names:
            act(
                pltpu.make_async_copy(
                    (q_ref, k_ref, v_ref)[which].at[:, lanes],
                    streams.at[slot, which],
                    in_sem.at[slot, which],
                )
            )

    fetch(0, (0, 1, 2), lambda copy: copy.start())
    weight_copy = pltpu.make_async_copy(w_ref, block_of(ctx), wown_sem)
    weight_copy.start()

    barrier = pltpu.get_barrier_semaphore()

    @pl.when(z > 0)
    def _():
        pl.semaphore_signal(barrier, inc=1, device_id={"chan": targets[0]}, device_id_type=MESH)

    @pl.when(z < line - 1)
    def _():
        pl.semaphore_signal(barrier, inc=1, device_id={"chan": targets[1]}, device_id_type=MESH)

    pl.semaphore_signal(barrier, inc=1, device_id={"chan": targets[2]}, device_id_type=MESH)
    partners = [1] + list(range(2, blocks, 2))
    for by in range(1, blocks):
        pl.semaphore_signal(barrier, inc=1, device_id={"ctx": flip(by)}, device_id_type=MESH)
    lines = jnp.where(z > 0, 1, 0) + jnp.where(z < line - 1, 1, 0)
    pl.semaphore_wait(barrier, lines + blocks)

    def piece_copy(shard, piece, way):
        part = held.at[shard, piece]
        return pltpu.make_async_remote_copy(
            src_ref=part,
            dst_ref=part,
            send_sem=send_sem.at[shard, piece, way],
            recv_sem=recv_sem.at[shard, piece],
            device_id={"chan": targets[way]},
            device_id_type=MESH,
        )

    def weight_send(block, by, slot):
        return pltpu.make_async_remote_copy(
            src_ref=block_of(block),
            dst_ref=block_of(block),
            send_sem=wsend_sem.at[slot],
            recv_sem=wrecv_sem.at[block],
            device_id={"ctx": flip(by)},
            device_id_type=MESH,
        )

    def onward(code, piece, act):
        shard = code % shards
        flags = code // shards
        flags = jnp.where(piece < PIECES // 2, flags % 8, flags // 8)
        for way, bit in ((0, flags % 2), (1, (flags // 2) % 2), (2, flags // 4)):

            @pl.when(bit == 1)
            def _(way=way):
                act(piece_copy(shard, piece, way))

    def ends_copy(source, piece, by):
        part = ends.at[source, piece]
        return pltpu.make_async_remote_copy(
            src_ref=part,
            dst_ref=part,
            send_sem=esend_sem.at[piece, by],
            recv_sem=erecv_sem.at[source, piece],
            device_id={"ctx": flip(by)},
            device_id_type=MESH,
        )

    def places(piece, sub):
        chunk = piece * per_piece + sub
        lanes = pl.ds(pl.multiple_of(chunk * LANES, LANES), LANES)
        inside = pl.ds(pl.multiple_of(sub * LANES, LANES), LANES)
        return chunk, lanes, inside

    def advance(chunk, names):
        @pl.when(chunk < chunks - 1)
        def _():
            fetch(chunk + 1, names, lambda copy: copy.start())

        fetch(chunk, names, lambda copy: copy.wait())

    def end_piece(piece):
        @pl.loop(0, per_piece)
        def _(sub):
            chunk, lanes, inside = places(piece, sub)
            advance(chunk, (1, 2))
            end_chunk(
                [streams.at[chunk % 2, 1], streams.at[chunk % 2, 2]],
                edge_ref.at[:, :, lanes],
                taps_ref.at[:, :, lanes],
                rate_ref[:, lanes],
                total.at[:, lanes],
                segs.at[:, :, lanes],
                ends.at[ctx, piece, :, inside],
                padded, drive,
            )

        for by in range(1, blocks):
            ends_copy(ctx, piece, by).start()

    def gate_piece(piece):
        for by in range(1, blocks):
            ends_copy(flip(by), piece, by).wait_recv()

        @pl.loop(0, per_piece)
        def _(sub):
            chunk, lanes, inside = places(piece, sub)
            advance(chunk, (0,))
            rate = rate_ref[:, lanes]
            carry = jnp.zeros(rate.shape, jnp.float32)
            for source in range(blocks):
                hops = ctx - 1 - source
                span = (tokens * jnp.maximum(hops, 0)).astype(jnp.float32)
                part = jnp.exp(-rate * span) * ends[source, piece, :, inside]
                carry = carry + jnp.where(hops >= 0, part, 0.0)
            gate_chunk(
                streams.at[chunk % 2, 0],
                edge_ref.at[:, :, lanes],
                taps_ref.at[:, :, lanes],
                rate,
                gain_ref[:, lanes],
                skip_ref[:, lanes],
                segs.at[:, :, lanes],
                carry,
                total.at[:, lanes],
                held.at[me, piece, :, inside],
                padded, drive, query, conv, starts,
            )

        onward(codes[0], piece, lambda copy: copy.start())

    @pl.loop(0, PIECES + 1)
    def _(step):
        @pl.when(step < PIECES)
        def _():
            end_piece(step)

        @pl.when(step >= 1)
        def _():
            gate_piece(step - 1)

    weight_copy.wait()
    first_sends = [weight_send(ctx, by, slot) for slot, by in enumerate(partners)]
    for copy in first_sends:
        copy.start()

    def zero_rows(at):
        total[pl.ds(pl.multiple_of(at * 64, 64), 64), :] = jnp.zeros((64, columns), jnp.float32)

    pl.loop(0, tokens // 64)(zero_rows)

    def arrive(code, piece):
        piece_copy(code % shards, piece, 2).wait_recv()
        onward(code, piece, lambda copy: copy.start())

    half = shards // 2
    later_sends = []
    for k in range(1, half):

        @pl.loop(0, PIECES)
        def _(piece, code=codes[k]):
            arrive(code, piece)

    for by in partners[1:]:
        block = flip(by)
        weight_send(block, 1, 0).wait_recv()
        copy = weight_send(block, 1, len(partners) + len(later_sends))
        copy.start()
        later_sends.append(copy)

    weight_send(flip(1), 1, 0).wait_recv()
    for by in partners[1:]:
        weight_send(flip(by + 1), 1, 0).wait_recv()

    tile = 256

    rows = tokens // 2

    def multiply(shard, piece):
        deep = pl.ds(pl.multiple_of(shard * channels + piece * width, width), width)

        @pl.loop(0, columns // tile)
        def _(part):
            cols = pl.ds(pl.multiple_of(part * tile, tile), tile)
            for at in range(0, tokens, rows):
                total[at : at + rows, cols] += jnp.dot(
                    held[shard, piece, at : at + rows, :],
                    weight[deep, cols],
                    preferred_element_type=jnp.float32,
                )

    @pl.loop(half, shards)
    def _(k):
        code = pick(codes, k)
        earlier = pick(codes, 2 * (k - half)) % shards
        later = pick(codes, 2 * (k - half) + 1) % shards

        @pl.loop(0, PIECES)
        def _(piece):
            arrive(code, piece)
            multiply(earlier, piece)
            multiply(later, piece)

    def round_rows(at):
        here = pl.ds(pl.multiple_of(at * 64, 64), 64)
        out_ref[here, :] = total[here, :].astype(out_ref.dtype)

    pl.loop(0, tokens // 64)(round_rows)

    @pl.loop(0, shards)
    def _(k):
        code = pick(codes, k)

        @pl.loop(0, PIECES)
        def _(piece):
            onward(code, piece, lambda copy: copy.wait_send())

    for copy in first_sends + later_sends:
        copy.wait_send()
    for piece in range(PIECES):
        for by in range(1, blocks):
            ends_copy(ctx, piece, by).wait_send()


def on_device(query_in, key_in, value_in, short_filter, residue, decay_rate, skip_gain, out_weight):
    tokens, channels = query_in.shape
    tap_count = short_filter.shape[1]
    modes = decay_rate.shape[1]
    shards = lax.axis_size("chan")
    blocks = lax.axis_size("ctx")
    edge = jnp.stack([x[tokens - (tap_count - 1) :, :] for x in (query_in, key_in, value_in)])
    edge = lax.ppermute(edge, "ctx", [(i, i + 1) for i in range(blocks - 1)])
    edge = edge.astype(jnp.float32)
    rate = decay_rate.T
    gain = (residue * jnp.sqrt(decay_rate)).T
    skip = skip_gain[None, :]

    flat = pltpu.VMEM((tokens, LANES), jnp.float32)
    pad = pltpu.VMEM((tokens + HALO, LANES), jnp.float32)
    work = tokens * channels * modes
    depth, columns = out_weight.shape
    partners = blocks // 2
    return pl.pallas_call(
        functools.partial(mix_kernel, shards, blocks),
        in_specs=[pl.BlockSpec(memory_space=pl.ANY)] * 4
        + [pl.BlockSpec(memory_space=pltpu.VMEM)] * 5,
        out_specs=pl.BlockSpec(memory_space=pltpu.VMEM),
        out_shape=jax.ShapeDtypeStruct((tokens, columns), jnp.bfloat16),
        scratch_shapes=[
            pltpu.VMEM((shards, PIECES, tokens, channels // PIECES), jnp.bfloat16),
            pltpu.VMEM((blocks * depth, columns), jnp.bfloat16),
            pltpu.VMEM((tokens, columns), jnp.float32),
            pltpu.VMEM((2, 3, tokens, LANES), jnp.bfloat16),
            pad,
            flat,
            flat,
            flat,
            pltpu.VMEM((modes, SEGMENTS, LANES), jnp.float32),
            pltpu.VMEM((modes, SEGMENTS, channels), jnp.float32),
            pltpu.VMEM((blocks, PIECES, modes, channels // PIECES), jnp.float32),
            pltpu.SemaphoreType.DMA((2, 3)),
            pltpu.SemaphoreType.DMA((PIECES, blocks)),
            pltpu.SemaphoreType.DMA((blocks, PIECES)),
            pltpu.SemaphoreType.DMA,
            pltpu.SemaphoreType.DMA((shards, PIECES, 3)),
            pltpu.SemaphoreType.DMA((shards, PIECES)),
            pltpu.SemaphoreType.DMA((2 * partners,)),
            pltpu.SemaphoreType.DMA((blocks,)),
        ],
        compiler_params=pltpu.CompilerParams(
            collective_id=0, has_side_effects=True, vmem_limit_bytes=62 * MIB
        ),
        cost_estimate=pl.CostEstimate(
            flops=2 * tokens * shards * channels * columns + 6 * work,
            bytes_accessed=6 * tokens * channels + 2 * depth * columns + 2 * tokens * columns,
            transcendentals=0,
        ),
        name="mix",
    )(
        query_in, key_in, value_in, out_weight, edge, short_filter, rate, gain, skip,
    )


def solution(mesh):
    in_specs = (
        P("ctx", "chan"),
        P("ctx", "chan"),
        P("ctx", "chan"),
        P(None, None, "chan"),
        P("chan", None),
        P("chan", None),
        P("chan"),
        P("ctx", "chan"),
    )
    return jax.shard_map(
        on_device, mesh=mesh, in_specs=in_specs, out_specs=P("ctx", "chan"), check_vma=False
    )
```
